256 devices in a mesh: row: 8 (over x_lo, y), col: 16 (over z, x_hi), dp: 2 (over core).
Axes of the slice: x: 4 (x_hi: 2, x_lo: 2; x = x_hi * 2 + x_lo), y: 4, z: 8, core: 2. Of those that a mesh axis runs over, the one named last changes fastest.
Arguments:
- tokens: bfloat16 [1024, 8192], P(('row', 'dp'), 'col'), may hold values from -6 to 6
- upstream: bfloat16 [1024, 8192], P(('row', 'dp'), 'col'), may hold values from -1.5 to 1.5
- w_gate: bfloat16 [8192, 14336], P('col', 'row'), may hold values from -0.0625 to 0.0625
- w_up: bfloat16 [8192, 14336], P('col', 'row'), may hold values from -0.0625 to 0.0625
- w_down: bfloat16 [14336, 8192], P('row', 'col'), may hold values from -0.046875 to 0.046875
- delta_gate: bfloat16 [16, 8, 24, 128, 128], P('col', 'row'), may hold values from -0.03125 to 0.03125
- delta_up: bfloat16 [16, 8, 24, 128, 128], P('col', 'row'), may hold values from -0.03125 to 0.03125
- delta_down: bfloat16 [8, 16, 24, 128, 128], P('row', 'col'), may hold values from -0.0234375 to 0.0234375
- pattern_gate: int32 [16, 8, 24], P('col', 'row'), may hold values from 0 to 56, as said below
- pattern_up: int32 [16, 8, 24], P('col', 'row'), may hold values from 0 to 56, as said below
- pattern_down: int32 [8, 16, 24], P('row', 'col'), may hold values from 0 to 56, as said below
Outputs:
- output: bfloat16 [1024, 8192], P(('row', 'dp'), 'col')
- input_grad: bfloat16 [1024, 8192], P(('row', 'dp'), 'col')
- delta_grad_gate: float32 [16, 8, 24, 128, 128], P('col', 'row', 'dp')
- delta_grad_up: float32 [16, 8, 24, 128, 128], P('col', 'row', 'dp')
- delta_grad_down: float32 [8, 16, 24, 128, 128], P('row', 'col', 'dp')
The draws below stay inside these ranges and needn't reach their ends.
Inputs may be any that keep to these rules, and one draw needn't show every extreme that they name: `pattern_gate`: in each tile the 24 slots name distinct blocks of that tile; the value 56 marks an empty slot; live slots come first, a tile holds 6 to 24 of them, and some tile holds 24. `pattern_up`: as for pattern_gate. `pattern_down`: as for pattern_gate.
All inputs are finite; a program needn't handle non-finite values.
Results may differ from the reference program's by a relative error of at most 0.0058.
Values may be sent and summed in bfloat16 or wider, within the bound.
No kernel may reach another device: no remote copies, remote signals or barrier semaphores. Data moves between devices by JAX's collectives and lax.ppermute only.
A program may use at most 128 MiB of HBM per device.

```python
import jax
import jax.numpy as jnp
from jax import lax

D = 8192
FF = 14336
BLK = 128
TOKENS = 1024
TILE_BLOCKS = 56
CAP = 24
N_ROW = 8
N_COL = 16


def make_pattern(base_key, tiles_first, tiles_second):
    count_key, full_key, score_key = jax.random.split(base_key, 3)
    tile_total = tiles_first * tiles_second
    counts = jax.random.randint(count_key, (tile_total,), CAP // 4, CAP + 1, dtype=jnp.int32)
    filled = jax.random.randint(full_key, (), 0, tile_total, dtype=jnp.int32)
    counts = jnp.where(jnp.arange(tile_total, dtype=jnp.int32) == filled, CAP, counts)
    scores = jax.random.randint(score_key, (tile_total, TILE_BLOCKS), 0, 1 << 20, dtype=jnp.int32) * TILE_BLOCKS
    scores = scores + jnp.arange(TILE_BLOCKS, dtype=jnp.int32)[None, :]
    ranking = jnp.argsort(scores, axis=1, stable=True).astype(jnp.int32)
    chosen = ranking[:, :CAP]
    live = jnp.arange(CAP, dtype=jnp.int32)[None, :] < counts[:, None]
    pattern = jnp.where(live, chosen, TILE_BLOCKS)
    return pattern.reshape(tiles_first, tiles_second, CAP).astype(jnp.int32)


def draw_pattern_gate(key, part):
    return make_pattern(jax.random.fold_in(key, 11), N_COL, N_ROW)


def draw_pattern_up(key, part):
    return make_pattern(jax.random.fold_in(key, 12), N_COL, N_ROW)


def draw_pattern_down(key, part):
    return make_pattern(jax.random.fold_in(key, 13), N_ROW, N_COL)


def block_scale(rng, dims, cuts, smallest, largest):
    gain, own = 1.0, jax.random.fold_in(rng, 6)
    for dim, blocks in cuts:
        heights = jnp.exp(jax.random.uniform(jax.random.fold_in(own, dim), (blocks,), jnp.float32, smallest / len(cuts), largest / len(cuts)))
        gain = gain * jnp.repeat(heights, dims[dim] // blocks).reshape([-1 if axis == dim else 1 for axis in range(len(dims))])
    return gain


def gaussian(key, shape, scale, reach, shards=(), held_as=jnp.bfloat16):
    entries = scale * jax.random.normal(key, shape, jnp.float32)
    if shards:
        entries = entries * block_scale(key, shape, shards, -0.22, 0.18)
    return jnp.clip(entries, -reach, reach).astype(held_as)


def setup_inputs(seed: int = 0) -> dict:
    arg_keys = jax.random.split(jax.random.key(seed), 12)
    tokens = gaussian(arg_keys[0], (TOKENS, D), 1.0, 6.0, ((0, 16), (1, 16)))
    upstream = gaussian(arg_keys[1], (TOKENS, D), 0.25, 1.5, ((0, 16), (1, 16)))
    w_gate = gaussian(arg_keys[2], (D, FF), D ** -0.5, 0.0625, ((0, 16), (1, 8)))
    w_up = gaussian(arg_keys[3], (D, FF), D ** -0.5, 0.0625, ((0, 16), (1, 8)))
    w_down = gaussian(arg_keys[4], (FF, D), FF ** -0.5, 0.046875, ((0, 8), (1, 16)))
    delta_gate = gaussian(arg_keys[5], (N_COL, N_ROW, CAP, BLK, BLK), (4 * D) ** -0.5, 0.03125, ((0, 16), (1, 8)))
    delta_up = gaussian(arg_keys[6], (N_COL, N_ROW, CAP, BLK, BLK), (4 * D) ** -0.5, 0.03125, ((0, 16), (1, 8)))
    delta_down = gaussian(arg_keys[7], (N_ROW, N_COL, CAP, BLK, BLK), (4 * FF) ** -0.5, 0.0234375, ((0, 8), (1, 16)))
    pattern_gate = draw_pattern_gate(jax.random.fold_in(arg_keys[11], 71), 0)
    pattern_up = draw_pattern_up(jax.random.fold_in(arg_keys[11], 71), 0)
    pattern_down = draw_pattern_down(jax.random.fold_in(arg_keys[11], 71), 0)
    return {"tokens": tokens, "upstream": upstream, "w_gate": w_gate, "w_up": w_up, "w_down": w_down, "delta_gate": delta_gate, "delta_up": delta_up, "delta_down": delta_down, "pattern_gate": pattern_gate, "pattern_up": pattern_up, "pattern_down": pattern_down}


def fold_whole(weight, blocks, pattern):
    tiles_first = blocks.shape[0]
    tiles_second = blocks.shape[1]
    block_size = blocks.shape[3]
    per_first = weight.shape[0] // (tiles_first * block_size)
    per_second = weight.shape[1] // (tiles_second * block_size)
    numbers = jnp.arange(per_first * per_second, dtype=jnp.int32)
    one_hot = (pattern[..., None] == numbers).astype(jnp.float32)
    placed = jnp.einsum("absk,absij->abkij", one_hot, blocks.astype(jnp.float32))
    placed = placed.reshape(tiles_first, tiles_second, per_first, per_second, block_size, block_size)
    placed = placed.transpose(0, 2, 4, 1, 3, 5).reshape(weight.shape)
    return (weight.astype(jnp.float32) + placed).astype(jnp.bfloat16)


def block_grads(left_rows, right_rows, pattern):
    tiles_first = pattern.shape[0]
    tiles_second = pattern.shape[1]
    block_size = BLK
    per_first = left_rows.shape[1] // (tiles_first * block_size)
    per_second = right_rows.shape[1] // (tiles_second * block_size)
    tile_blocks = per_first * per_second
    left_blocks = left_rows.reshape(left_rows.shape[0], tiles_first * per_first, block_size)
    right_blocks = right_rows.reshape(right_rows.shape[0], tiles_second * per_second, block_size)

    def one_tile(inputs):
        first_index, tile_pattern = inputs
        usable = (tile_pattern < tile_blocks).astype(jnp.float32)
        clipped = jnp.minimum(tile_pattern, tile_blocks - 1)
        left_index = first_index * per_first + clipped // per_second
        right_index = jnp.arange(tiles_second, dtype=jnp.int32)[:, None] * per_second + clipped % per_second
        left_pick = jnp.take(left_blocks, left_index, axis=1).astype(jnp.float32)
        right_pick = jnp.take(right_blocks, right_index, axis=1).astype(jnp.float32)
        result = jnp.einsum("tbsi,tbsj->bsij", left_pick, right_pick)
        return result * usable[:, :, None, None]

    return lax.map(one_tile, (jnp.arange(tiles_first, dtype=jnp.int32), pattern))


def reference(tokens, upstream, w_gate, w_up, w_down, delta_gate, delta_up, delta_down, pattern_gate, pattern_up, pattern_down):
    gate_folded = fold_whole(w_gate, delta_gate, pattern_gate)
    up_folded = fold_whole(w_up, delta_up, pattern_up)
    down_folded = fold_whole(w_down, delta_down, pattern_down)
    gate_all = jnp.dot(tokens, gate_folded, preferred_element_type=jnp.float32)
    up_all = jnp.dot(tokens, up_folded, preferred_element_type=jnp.float32)
    sigmoid_all = jax.nn.sigmoid(gate_all)
    hidden = (gate_all * sigmoid_all * up_all).astype(jnp.bfloat16)
    output = jnp.dot(hidden, down_folded, preferred_element_type=jnp.float32).astype(jnp.bfloat16)
    backward = jnp.dot(upstream, down_folded.T, preferred_element_type=jnp.float32)
    grad_gate = (backward * up_all * sigmoid_all * (1.0 + gate_all * (1.0 - sigmoid_all))).astype(jnp.bfloat16)
    grad_up = (backward * gate_all * sigmoid_all).astype(jnp.bfloat16)
    input_grad = (jnp.dot(grad_gate, gate_folded.T, preferred_element_type=jnp.float32)
                  + jnp.dot(grad_up, up_folded.T, preferred_element_type=jnp.float32)).astype(jnp.bfloat16)
    delta_grad_gate = block_grads(tokens, grad_gate, pattern_gate)
    delta_grad_up = block_grads(tokens, grad_up, pattern_up)
    delta_grad_down = block_grads(hidden, upstream, pattern_down)
    return (output, input_grad, delta_grad_gate, delta_grad_up, delta_grad_down)
```

```python
import jax
import jax.numpy as jnp
from jax import lax
from jax.experimental import pallas as pl
from jax.experimental.pallas import tpu as pltpu
from jax.sharding import Mesh
from jax.sharding import PartitionSpec as P

ROW = ("xl", "y")
COL = ("z", "xh")
BF = jnp.bfloat16
F32 = jnp.float32
STEP = 256
VMEM_LIMIT = 48 * 1024 * 1024


def params():
    return pltpu.CompilerParams(vmem_limit_bytes=VMEM_LIMIT)


def cost(flops, moved):
    return pl.CostEstimate(flops=int(flops), bytes_accessed=int(moved), transcendentals=0)


def row_shift(value, dx, dy, sign):
    nx, ny = lax.axis_size("xl"), lax.axis_size("y")
    perm = [
        (a * ny + b, ((a + dx) % nx) * ny + (b + sign * dy) % ny)
        for a in range(nx)
        for b in range(ny)
    ]
    return lax.ppermute(value, ROW, perm)


def row_offsets():
    nx, ny = lax.axis_size("xl"), lax.axis_size("y")
    return [(dx, dy) for dx in range(nx) for dy in range(ny)]


def row_gather(value):
    return [
        value if (dx, dy) == (0, 0) else row_shift(value, dx, dy, 1) for dx, dy in row_offsets()
    ]


def row_sum(parts):
    total = parts[0].astype(F32)
    for (dx, dy), part in list(zip(row_offsets(), parts))[1:]:
        total = total + row_shift(part, dx, dy, -1).astype(F32)
    return total


def z_shift(value, by):
    n = lax.axis_size("z")
    return lax.ppermute(value, "z", [(i, (i + by) % n) for i in range(n)])


def z_sum(partial):
    n, _, width = partial.shape
    me = lax.axis_index("z")
    half, far = width // 2, n // 2

    def part(d):
        return lax.dynamic_index_in_dim(partial, (me + d) % n, 0, keepdims=False)

    opposite = part(far)
    up = z_shift(opposite[:, :half].astype(BF), 1)
    down = z_shift(opposite[:, half:].astype(BF), -1)
    up_term, down_term = part(far - 1), part(1 - far)
    up_send = jnp.concatenate((up_term[:, :half] + up.astype(F32), up_term[:, half:]), axis=1)
    down_send = jnp.concatenate(
        (down_term[:, :half], down_term[:, half:] + down.astype(F32)), axis=1
    )
    for d in range(far - 1, 0, -1):
        up = z_shift(up_send.astype(BF), 1)
        down = z_shift(down_send.astype(BF), -1)
        if d > 1:
            up_send = part(d - 1) + up.astype(F32)
            down_send = part(1 - d) + down.astype(F32)
    return part(0) + up.astype(F32) + down.astype(F32)


def z_gather(value):
    n = lax.axis_size("z")
    half, far = value.shape[1] // 2, n // 2
    pieces, below, above = [value], value, value
    for _ in range(far - 1):
        below, above = z_shift(below, 1), z_shift(above, -1)
        pieces += [below, above]
    return pieces + [z_shift(below[:, :half], 1), z_shift(above[:, half:], -1)]


def xh_add(value):
    other = lax.ppermute(value.astype(BF), "xh", [(0, 1), (1, 0)])
    return value + other.astype(F32)


def fold_kernel(pattern, w_ref, blocks_ref, out_ref):
    size = blocks_ref.shape[-1]
    down = out_ref.shape[0] // size
    across = out_ref.shape[1] // size
    out_ref[...] = w_ref[...]

    def one(s, carry):
        k = pattern[s]

        @pl.when(k < down * across)
        def _():
            rows = pl.ds(pl.multiple_of((k // across) * size, size), size)
            columns = pl.ds(pl.multiple_of((k % across) * size, size), size)
            total = w_ref[rows, columns].astype(F32) + blocks_ref[s].astype(F32)
            out_ref[rows, columns] = total.astype(BF)

        return carry

    lax.fori_loop(0, blocks_ref.shape[0], one, 0)


def fold(weight, blocks, pattern):
    slots, size = blocks.shape[2], blocks.shape[3]
    return pl.pallas_call(
        fold_kernel,
        out_shape=jax.ShapeDtypeStruct(weight.shape, BF),
        in_specs=[
            pl.BlockSpec(memory_space=pltpu.SMEM),
            pl.BlockSpec(memory_space=pltpu.VMEM),
            pl.BlockSpec(memory_space=pltpu.VMEM),
        ],
        out_specs=pl.BlockSpec(memory_space=pltpu.VMEM),
        compiler_params=params(),
        cost_estimate=cost(weight.size, weight.size * 4 + blocks.size * 2),
        name="fold",
    )(pattern.reshape(-1), weight, blocks.reshape(slots, size, size))


def start_rows(pieces, whole, sems):
    copies = []
    rows = pieces[0].shape[0]
    for d, piece in enumerate(pieces):
        copies.append(pltpu.make_async_copy(piece, whole.at[pl.ds(d * rows, rows)], sems.at[d]))
    for c in copies:
        c.start()
    return copies


def start_ring(pieces, whole, sems, me):
    rows, width = pieces[0].shape
    n = whole.shape[0] // rows
    half = width // 2
    spots = [0]
    for d in range(1, n // 2):
        spots += [-d, d]
    copies = []
    for at, d in enumerate(spots):
        to = pl.ds(pl.multiple_of(((me + d + n) % n) * rows, rows), rows)
        copies.append(pltpu.make_async_copy(pieces[at], whole.at[to], sems.at[at]))
    to = pl.ds(pl.multiple_of(((me + n // 2) % n) * rows, rows), rows)
    copies.append(pltpu.make_async_copy(pieces[n - 1], whole.at[to, pl.ds(0, half)], sems.at[n - 1]))
    copies.append(pltpu.make_async_copy(pieces[n], whole.at[to, pl.ds(half, half)], sems.at[n]))
    for c in copies:
        c.start()
    return copies


def first_products(pieces, weights, transposed):
    n = len(pieces)
    rows, depth = pieces[0].shape
    m = n * rows
    count = len(weights)
    width = weights[0].shape[0 if transposed else 1]
    dims = (((1,), (1 if transposed else 0,)), ((), ()))

    def kernel(*refs):
        pieces_in, w, outs = refs[:n], refs[n : n + count], refs[n + count : n + 2 * count]
        whole, sems = refs[n + 2 * count :]

        @pl.when(pl.program_id(0) == 0)
        def _():
            for c in start_rows(pieces_in, whole, sems):
                c.wait()

        for w_ref, o_ref in zip(w, outs):
            o_ref[...] = lax.dot_general(
                whole[...], w_ref[...], dims, preferred_element_type=F32
            )

    if transposed:
        w_spec = pl.BlockSpec((STEP, depth), lambda i: (i, 0))
    else:
        w_spec = pl.BlockSpec((depth, STEP), lambda i: (0, i))
    return pl.pallas_call(
        kernel,
        grid=(width // STEP,),
        out_shape=[jax.ShapeDtypeStruct((m, width), F32)] * count,
        in_specs=[pl.BlockSpec(memory_space=pl.ANY)] * n + [w_spec] * count,
        out_specs=[pl.BlockSpec((m, STEP), lambda i: (0, i))] * count,
        scratch_shapes=[pltpu.VMEM((m, depth), BF), pltpu.SemaphoreType.DMA((n,))],
        compiler_params=params(),
        cost_estimate=cost(
            2 * m * depth * width * count, count * (depth * width * 2 + m * width * 4)
        ),
        name="first_products",
    )(*pieces, *weights)


def second_product(sides, weights, transposed):
    count = len(sides)
    n = len(sides[0])
    rows, depth = sides[0][0].shape
    m = (n - 1) * rows
    width = weights[0].shape[0 if transposed else 1]
    dims = (((1,), (1 if transposed else 0,)), ((), ()))
    steps = depth // STEP

    def kernel(*refs):
        pieces = [refs[s * n : (s + 1) * n] for s in range(count)]
        w = refs[count * n : count * n + count]
        out, total = refs[count * n + count : count * n + count + 2]
        wholes = refs[count * n + count + 2 : count * n + 2 * count + 2]
        sems = refs[-1]
        step = pl.program_id(0)

        @pl.when(step == 0)
        def _():
            me = lax.axis_index("z")
            copies = []
            for s in range(count):
                copies += start_ring(pieces[s], wholes[s], sems.at[s], me)
            for c in copies:
                c.wait()
            total[...] = jnp.zeros_like(total)

        acc = total[...]
        at = pl.ds(pl.multiple_of(step * STEP, STEP), STEP)
        for s in range(count):
            acc = acc + lax.dot_general(
                wholes[s][:, at], w[s][...], dims, preferred_element_type=F32
            )
        total[...] = acc

        @pl.when(step == steps - 1)
        def _():
            out[...] = total[...].astype(BF)

    if transposed:
        w_spec = pl.BlockSpec((width, STEP), lambda i: (0, i))
    else:
        w_spec = pl.BlockSpec((STEP, width), lambda i: (i, 0))
    return pl.pallas_call(
        kernel,
        grid=(steps,),
        out_shape=jax.ShapeDtypeStruct((m, width), BF),
        in_specs=[pl.BlockSpec(memory_space=pl.ANY)] * (count * n) + [w_spec] * count,
        out_specs=pl.BlockSpec((m, width), lambda i: (0, 0)),
        scratch_shapes=[pltpu.VMEM((m, width), F32)]
        + [pltpu.VMEM((m, depth), BF)] * count
        + [pltpu.SemaphoreType.DMA((count, n))],
        compiler_params=params(),
        cost_estimate=cost(
            2 * m * depth * width * count, count * (depth * width * 2 + m * depth * 2)
        ),
        name="second_product",
    )(*[p for side in sides for p in side], *weights)


def slot_grads(row_pieces, ring_pieces, pattern, size, ring_left):
    nr, nz = len(row_pieces), len(ring_pieces)
    rows, narrow = row_pieces[0].shape
    wide = ring_pieces[0].shape[1]
    m = nr * rows
    slots = pattern.size
    keep = slots // 2
    blocks = wide // size
    per_narrow = narrow // size
    contract = (((0,), (0,)), ((), ()))
    per_step = STEP // size

    def kernel(*refs):
        pattern_ref = refs[0]
        rp, zp = refs[1 : 1 + nr], refs[1 + nr : 1 + nr + nz]
        mine, send, whole_r, whole_z, dense, sems_r, sems_z = refs[1 + nr + nz :]
        me = lax.axis_index("z")
        copies = start_rows(rp, whole_r, sems_r) + start_ring(zp, whole_z, sems_z, me)
        for c in copies:
            c.wait()

        def tile(i, carry):
            at = pl.ds(pl.multiple_of(i * STEP, STEP), STEP)
            if ring_left:
                got = lax.dot_general(
                    whole_z[:, at], whole_r[...], contract, preferred_element_type=F32
                )
                dense[pl.ds(i * per_step, per_step)] = got.reshape(per_step, size, narrow)
            else:
                got = lax.dot_general(
                    whole_r[...], whole_z[:, at], contract, preferred_element_type=F32
                )
                for b in range(per_step):
                    dense[i * per_step + b] = got[:, b * size : (b + 1) * size]
            return carry

        lax.fori_loop(0, wide // STEP, tile, 0)
        core = lax.axis_index("dp")

        def pick(s):
            k = pattern_ref[s]
            live = k < blocks * per_narrow
            k = jnp.minimum(k, blocks * per_narrow - 1)
            if ring_left:
                a, b = k // per_narrow, k % per_narrow
                got = dense[a, :, pl.ds(pl.multiple_of(b * size, size), size)]
            else:
                a, b = k // blocks, k % blocks
                got = dense[b, pl.ds(pl.multiple_of(a * size, size), size), :]
            return jnp.where(live, got, jnp.zeros_like(got))

        def one(s, carry):
            mine[s] = pick(core * keep + s)
            send[s] = pick((1 - core) * keep + s).astype(send.dtype)
            return carry

        lax.fori_loop(0, keep, one, 0)

    dense_shape = (blocks, size, narrow) if ring_left else (blocks, narrow, size)
    out = (keep, size, size)
    return pl.pallas_call(
        kernel,
        out_shape=[jax.ShapeDtypeStruct(out, F32), jax.ShapeDtypeStruct(out, F32)],
        in_specs=[pl.BlockSpec(memory_space=pltpu.SMEM)]
        + [pl.BlockSpec(memory_space=pl.ANY)] * (nr + nz),
        out_specs=[pl.BlockSpec(memory_space=pltpu.VMEM)] * 2,
        scratch_shapes=[
            pltpu.VMEM((m, narrow), BF),
            pltpu.VMEM((m, wide), BF),
            pltpu.VMEM(dense_shape, F32),
            pltpu.SemaphoreType.DMA((nr,)),
            pltpu.SemaphoreType.DMA((nz,)),
        ],
        compiler_params=params(),
        cost_estimate=cost(2 * m * narrow * wide, m * (narrow + wide) * 2 + slots * size * size * 4),
        name="slot_grads",
    )(pattern.reshape(-1), *row_pieces, *ring_pieces)


def core_sum(mine, send):
    got = lax.ppermute(send, "dp", [(0, 1), (1, 0)])
    total = mine + got
    return total.reshape((1, 1) + total.shape)


def local(
    tokens,
    upstream,
    w_gate,
    w_up,
    w_down,
    delta_gate,
    delta_up,
    delta_down,
    pattern_gate,
    pattern_up,
    pattern_down,
):
    size = delta_gate.shape[-1]
    nz = lax.axis_size("z")
    token_pieces = row_gather(tokens)
    upstream_pieces = row_gather(upstream)
    gate_folded = fold(w_gate, delta_gate, pattern_gate)
    up_folded = fold(w_up, delta_up, pattern_up)
    down_folded = fold(w_down, delta_down, pattern_down)

    gate_part, up_part = first_products(token_pieces, (gate_folded, up_folded), False)
    (backward_part,) = first_products(upstream_pieces, (down_folded,), True)

    def column_sum(part):
        return xh_add(z_sum(part.reshape(nz, -1, part.shape[1])))

    gate = column_sum(gate_part)
    up = column_sum(up_part)
    s = jax.nn.sigmoid(gate)
    hidden = (gate * s * up).astype(BF)
    hidden_pieces = z_gather(hidden)

    backward = column_sum(backward_part)
    grad_gate = (backward * up * s * (1.0 + gate * (1.0 - s))).astype(BF)
    grad_up = (backward * gate * s).astype(BF)
    grad_up_pieces = z_gather(grad_up)
    grad_gate_pieces = z_gather(grad_gate)

    def back_to_rows(partial):
        return row_sum(list(partial.reshape(len(token_pieces), -1, partial.shape[1]))).astype(BF)

    output = back_to_rows(second_product((hidden_pieces,), (down_folded,), False))
    delta_grad_down = core_sum(
        *slot_grads(upstream_pieces, hidden_pieces, pattern_down, size, True)
    )
    input_grad = back_to_rows(
        second_product((grad_gate_pieces, grad_up_pieces), (gate_folded, up_folded), True)
    )
    delta_grad_up = core_sum(*slot_grads(token_pieces, grad_up_pieces, pattern_up, size, False))
    delta_grad_gate = core_sum(
        *slot_grads(token_pieces, grad_gate_pieces, pattern_gate, size, False)
    )
    return (output, input_grad, delta_grad_gate, delta_grad_up, delta_grad_down)


def solution(mesh):
    finer = Mesh(
        mesh.devices.reshape(2, mesh.shape["row"] // 2, mesh.shape["col"] // 2, 2, 2),
        ("xl", "y", "z", "xh", "dp"),
    )
    placed = (
        P(("xl", "y", "dp"), COL),
        P(("xl", "y", "dp"), COL),
        P(COL, ROW),
        P(COL, ROW),
        P(ROW, COL),
        P(COL, ROW, None, None, None),
        P(COL, ROW, None, None, None),
        P(ROW, COL, None, None, None),
        P(COL, ROW, None),
        P(COL, ROW, None),
        P(ROW, COL, None),
    )
    return jax.shard_map(
        local,
        mesh=finer,
        in_specs=placed,
        out_specs=(
            P(("xl", "y", "dp"), COL),
            P(("xl", "y", "dp"), COL),
            P(COL, ROW, "dp", None, None),
            P(COL, ROW, "dp", None, None),
            P(ROW, COL, "dp", None, None),
        ),
        check_vma=False,
    )
```

```python
import jax
import jax.numpy as jnp
from jax import lax
from jax.experimental import pallas as pl
from jax.experimental.pallas import tpu as pltpu
from jax.sharding import Mesh
from jax.sharding import PartitionSpec as P

ROW = ("xl", "y")
COL = ("z", "xh")
BF = jnp.bfloat16
F32 = jnp.float32
STEP = 256
VMEM_LIMIT = 48 * 1024 * 1024


def params():
    return pltpu.CompilerParams(vmem_limit_bytes=VMEM_LIMIT)


def cost(flops, moved):
    return pl.CostEstimate(flops=int(flops), bytes_accessed=int(moved), transcendentals=0)


def row_shift(value, dx, dy, sign):
    nx, ny = lax.axis_size("xl"), lax.axis_size("y")
    perm = [
        (a * ny + b, ((a + dx) % nx) * ny + (b + sign * dy) % ny)
        for a in range(nx)
        for b in range(ny)
    ]
    return lax.ppermute(value, ROW, perm)


def row_offsets():
    nx, ny = lax.axis_size("xl"), lax.axis_size("y")
    return [(dx, dy) for dx in range(nx) for dy in range(ny)]


def row_behind(dx, dy):
    nx, ny = lax.axis_size("xl"), lax.axis_size("y")
    return ((lax.axis_index("xl") + nx - dx) % nx) * ny + (lax.axis_index("y") + ny - dy) % ny


def row_gather(value):
    return [
        value if (dx, dy) == (0, 0) else row_shift(value, dx, dy, 1) for dx, dy in row_offsets()
    ]


def row_sum(parts):
    total = None
    for dx, dy in row_offsets():
        part = lax.dynamic_index_in_dim(parts, row_behind(dx, dy), 0, keepdims=False)
        if (dx, dy) != (0, 0):
            part = row_shift(part, dx, dy, -1)
        total = part.astype(F32) if total is None else total + part.astype(F32)
    return total


def z_shift(value, by):
    n = lax.axis_size("z")
    return lax.ppermute(value, "z", [(i, (i + by) % n) for i in range(n)])


def z_sum(partial):
    n, _, width = partial.shape
    me = lax.axis_index("z")
    half, far = width // 2, n // 2

    def part(d):
        return lax.dynamic_index_in_dim(partial, (me + d) % n, 0, keepdims=False)

    opposite = part(far)
    up = z_shift(opposite[:, :half].astype(BF), 1)
    down = z_shift(opposite[:, half:].astype(BF), -1)
    up, down = lax.optimization_barrier((up, down))
    up_term, down_term = part(far - 1), part(1 - far)
    up_send = jnp.concatenate((up_term[:, :half] + up.astype(F32), up_term[:, half:]), axis=1)
    down_send = jnp.concatenate(
        (down_term[:, :half], down_term[:, half:] + down.astype(F32)), axis=1
    )
    for d in range(far - 1, 0, -1):
        up = z_shift(up_send.astype(BF), 1)
        down = z_shift(down_send.astype(BF), -1)
        up, down = lax.optimization_barrier((up, down))
        if d > 1:
            up_send = part(d - 1) + up.astype(F32)
            down_send = part(1 - d) + down.astype(F32)
    return part(0) + up.astype(F32) + down.astype(F32)


def z_gather(value):
    n = lax.axis_size("z")
    half, far = value.shape[1] // 2, n // 2
    pieces, below, above = [value], value, value
    for _ in range(far - 1):
        below, above = z_shift(below, 1), z_shift(above, -1)
        below, above = lax.optimization_barrier((below, above))
        pieces += [below, above]
    return pieces + [z_shift(below[:, :half], 1), z_shift(above[:, half:], -1)]


def xh_add(value):
    other = lax.ppermute(value.astype(BF), "xh", [(0, 1), (1, 0)])
    return value + other.astype(F32)


def fold_kernel(pattern, w_ref, blocks_ref, out_ref):
    size = blocks_ref.shape[-1]
    down = out_ref.shape[0] // size
    across = out_ref.shape[1] // size
    out_ref[...] = w_ref[...]

    def one(s, carry):
        k = pattern[s]

        @pl.when(k < down * across)
        def _():
            rows = pl.ds(pl.multiple_of((k // across) * size, size), size)
            columns = pl.ds(pl.multiple_of((k % across) * size, size), size)
            total = w_ref[rows, columns].astype(F32) + blocks_ref[s].astype(F32)
            out_ref[rows, columns] = total.astype(BF)

        return carry

    lax.fori_loop(0, blocks_ref.shape[0], one, 0)


def fold(weight, blocks, pattern):
    slots, size = blocks.shape[2], blocks.shape[3]
    return pl.pallas_call(
        fold_kernel,
        out_shape=jax.ShapeDtypeStruct(weight.shape, BF),
        in_specs=[
            pl.BlockSpec(memory_space=pltpu.SMEM),
            pl.BlockSpec(memory_space=pltpu.VMEM),
            pl.BlockSpec(memory_space=pltpu.VMEM),
        ],
        out_specs=pl.BlockSpec(memory_space=pltpu.VMEM),
        compiler_params=params(),
        cost_estimate=cost(weight.size, weight.size * 4 + blocks.size * 2),
        name="fold",
    )(pattern.reshape(-1), weight, blocks.reshape(slots, size, size))


def start_rows(pieces, whole, sems):
    copies = []
    rows = pieces[0].shape[0]
    for d, (dx, dy) in enumerate(row_offsets()):
        to = pl.ds(pl.multiple_of(row_behind(dx, dy) * rows, rows), rows)
        copies.append(pltpu.make_async_copy(pieces[d], whole.at[to], sems.at[d]))
    for c in copies:
        c.start()
    return copies


def start_ring(pieces, whole, sems, me):
    rows, width = pieces[0].shape
    n = whole.shape[0] // rows
    half = width // 2
    spots = [0]
    for d in range(1, n // 2):
        spots += [-d, d]
    copies = []
    for at, d in enumerate(spots):
        to = pl.ds(pl.multiple_of(((me + d + n) % n) * rows, rows), rows)
        copies.append(pltpu.make_async_copy(pieces[at], whole.at[to], sems.at[at]))
    to = pl.ds(pl.multiple_of(((me + n // 2) % n) * rows, rows), rows)
    copies.append(pltpu.make_async_copy(pieces[n - 1], whole.at[to, pl.ds(0, half)], sems.at[n - 1]))
    copies.append(pltpu.make_async_copy(pieces[n], whole.at[to, pl.ds(half, half)], sems.at[n]))
    for c in copies:
        c.start()
    return copies


def first_products(pieces, weights):
    n = len(pieces)
    rows, depth = pieces[0].shape
    m = n * rows
    count = len(weights)
    width = weights[0].shape[1]

    def kernel(*refs):
        pieces_in, w, outs = refs[:n], refs[n : n + count], refs[n + count : n + 2 * count]
        whole, sems = refs[n + 2 * count :]

        @pl.when(pl.program_id(0) == 0)
        def _():
            for c in start_rows(pieces_in, whole, sems):
                c.wait()

        for w_ref, o_ref in zip(w, outs):
            o_ref[...] = jnp.dot(whole[...], w_ref[...], preferred_element_type=F32)

    return pl.pallas_call(
        kernel,
        grid=(width // STEP,),
        out_shape=[jax.ShapeDtypeStruct((m, width), F32)] * count
        + [jax.ShapeDtypeStruct((m, depth), BF)],
        in_specs=[pl.BlockSpec(memory_space=pl.ANY)] * n
        + [pl.BlockSpec((depth, STEP), lambda i: (0, i))] * count,
        out_specs=[pl.BlockSpec((m, STEP), lambda i: (0, i))] * count
        + [pl.BlockSpec((m, depth), lambda i: (0, 0))],
        scratch_shapes=[pltpu.SemaphoreType.DMA((n,))],
        compiler_params=params(),
        cost_estimate=cost(
            2 * m * depth * width * count, count * (depth * width * 2 + m * width * 4)
        ),
        name="first_products",
    )(*pieces, *weights)


def second_product(sides, weights, transposed):
    count = len(sides)
    n = len(sides[0])
    rows, depth = sides[0][0].shape
    m = (n - 1) * rows
    width = weights[0].shape[0 if transposed else 1]
    dims = (((1,), (1 if transposed else 0,)), ((), ()))
    steps = depth // STEP

    def kernel(*refs):
        pieces = [refs[s * n : (s + 1) * n] for s in range(count)]
        w = refs[count * n : count * n + count]
        out, total = refs[count * n + count : count * n + count + 2]
        wholes = refs[count * n + count + 2 : count * n + 2 * count + 2]
        sems = refs[-1]
        step = pl.program_id(0)

        @pl.when(step == 0)
        def _():
            me = lax.axis_index("z")
            copies = []
            for s in range(count):
                copies += start_ring(pieces[s], wholes[s], sems.at[s], me)
            for c in copies:
                c.wait()
            total[...] = jnp.zeros_like(total)

        acc = total[...]
        at = pl.ds(pl.multiple_of(step * STEP, STEP), STEP)
        for s in range(count):
            acc = acc + lax.dot_general(
                wholes[s][:, at], w[s][...], dims, preferred_element_type=F32
            )
        total[...] = acc

        @pl.when(step == steps - 1)
        def _():
            out[...] = total[...].astype(BF)

    if transposed:
        w_spec = pl.BlockSpec((width, STEP), lambda i: (0, i))
    else:
        w_spec = pl.BlockSpec((STEP, width), lambda i: (i, 0))
    return pl.pallas_call(
        kernel,
        grid=(steps,),
        out_shape=jax.ShapeDtypeStruct((m, width), BF),
        in_specs=[pl.BlockSpec(memory_space=pl.ANY)] * (count * n) + [w_spec] * count,
        out_specs=pl.BlockSpec((m, width), lambda i: (0, 0)),
        scratch_shapes=[pltpu.VMEM((m, width), F32)]
        + [pltpu.VMEM((m, depth), BF)] * count
        + [pltpu.SemaphoreType.DMA((count, n))],
        compiler_params=params(),
        cost_estimate=cost(
            2 * m * depth * width * count, count * (depth * width * 2 + m * depth * 2)
        ),
        name="second_product",
    )(*[p for side in sides for p in side], *weights)


def back_product(rows_all, weight):
    m, depth = rows_all.shape
    width = weight.shape[0]

    def kernel(rows_ref, w_ref, out_ref):
        out_ref[...] = lax.dot_general(
            rows_ref[...], w_ref[...], (((1,), (1,)), ((), ())), preferred_element_type=F32
        )

    return pl.pallas_call(
        kernel,
        grid=(width // STEP,),
        out_shape=jax.ShapeDtypeStruct((m, width), F32),
        in_specs=[
            pl.BlockSpec((m, depth), lambda i: (0, 0)),
            pl.BlockSpec((STEP, depth), lambda i: (i, 0)),
        ],
        out_specs=pl.BlockSpec((m, STEP), lambda i: (0, i)),
        compiler_params=params(),
        cost_estimate=cost(2 * m * depth * width, depth * width * 2 + m * width * 4),
        name="back_product",
    )(rows_all, weight)


def slot_grads(rows_all, ring_pieces, pattern, size, ring_left):
    nz = len(ring_pieces)
    m, narrow = rows_all.shape
    wide = ring_pieces[0].shape[1]
    slots = pattern.size
    keep = slots // 2
    blocks = wide // size
    per_narrow = narrow // size
    contract = (((0,), (0,)), ((), ()))
    per_step = STEP // size

    def kernel(*refs):
        pattern_ref = refs[0]
        whole_r, zp = refs[1], refs[2 : 2 + nz]
        mine, send, whole_z, dense, sems_z = refs[2 + nz :]
        for c in start_ring(zp, whole_z, sems_z, lax.axis_index("z")):
            c.wait()

        def tile(i, carry):
            at = pl.ds(pl.multiple_of(i * STEP, STEP), STEP)
            if ring_left:
                got = lax.dot_general(
                    whole_z[:, at], whole_r[...], contract, preferred_element_type=F32
                )
                dense[pl.ds(i * per_step, per_step)] = got.reshape(per_step, size, narrow)
            else:
                got = lax.dot_general(
                    whole_r[...], whole_z[:, at], contract, preferred_element_type=F32
                )
                for b in range(per_step):
                    dense[i * per_step + b] = got[:, b * size : (b + 1) * size]
            return carry

        lax.fori_loop(0, wide // STEP, tile, 0)
        core = lax.axis_index("dp")

        def pick(s):
            k = pattern_ref[s]
            live = k < blocks * per_narrow
            k = jnp.minimum(k, blocks * per_narrow - 1)
            if ring_left:
                a, b = k // per_narrow, k % per_narrow
                got = dense[a, :, pl.ds(pl.multiple_of(b * size, size), size)]
            else:
                a, b = k // blocks, k % blocks
                got = dense[b, pl.ds(pl.multiple_of(a * size, size), size), :]
            return jnp.where(live, got, jnp.zeros_like(got))

        def one(s, carry):
            mine[s] = pick(core * keep + s)
            send[s] = pick((1 - core) * keep + s).astype(send.dtype)
            return carry

        lax.fori_loop(0, keep, one, 0)

    dense_shape = (blocks, size, narrow) if ring_left else (blocks, narrow, size)
    out = (keep, size, size)
    return pl.pallas_call(
        kernel,
        out_shape=[jax.ShapeDtypeStruct(out, F32), jax.ShapeDtypeStruct(out, F32)],
        in_specs=[
            pl.BlockSpec(memory_space=pltpu.SMEM),
            pl.BlockSpec(memory_space=pltpu.VMEM),
        ]
        + [pl.BlockSpec(memory_space=pl.ANY)] * nz,
        out_specs=[pl.BlockSpec(memory_space=pltpu.VMEM)] * 2,
        scratch_shapes=[
            pltpu.VMEM((m, wide), BF),
            pltpu.VMEM(dense_shape, F32),
            pltpu.SemaphoreType.DMA((nz,)),
        ],
        compiler_params=params(),
        cost_estimate=cost(2 * m * narrow * wide, m * (narrow + wide) * 2 + slots * size * size * 4),
        name="slot_grads",
    )(pattern.reshape(-1), rows_all, *ring_pieces)


def core_sum(mine, send):
    got = lax.ppermute(send, "dp", [(0, 1), (1, 0)])
    total = mine + got
    return total.reshape((1, 1) + total.shape)


def local(
    tokens,
    upstream,
    w_gate,
    w_up,
    w_down,
    delta_gate,
    delta_up,
    delta_down,
    pattern_gate,
    pattern_up,
    pattern_down,
):
    size = delta_gate.shape[-1]
    nz = lax.axis_size("z")
    upstream_all = lax.all_gather(upstream, ROW, axis=0, tiled=True)
    token_pieces = row_gather(tokens)
    gate_folded = fold(w_gate, delta_gate, pattern_gate)
    up_folded = fold(w_up, delta_up, pattern_up)
    down_folded = fold(w_down, delta_down, pattern_down)

    gate_part, up_part, token_all = first_products(token_pieces, (gate_folded, up_folded))
    backward_part = back_product(upstream_all, down_folded)

    def column_sum(part):
        return xh_add(z_sum(part.reshape(nz, -1, part.shape[1])))

    gate = column_sum(gate_part)
    up = column_sum(up_part)
    s = jax.nn.sigmoid(gate)
    hidden = (gate * s * up).astype(BF)
    hidden_pieces = z_gather(hidden)

    backward = column_sum(backward_part)
    grad_up = (backward * gate * s).astype(BF)
    grad_gate = (backward * up * s * (1.0 + gate * (1.0 - s))).astype(BF)
    grad_up_pieces = z_gather(grad_up)
    grad_gate_pieces = z_gather(grad_gate)

    def back_to_rows(partial):
        return row_sum(partial.reshape(len(token_pieces), -1, partial.shape[1])).astype(BF)

    output = back_to_rows(second_product((hidden_pieces,), (down_folded,), False))
    delta_grad_down = core_sum(*slot_grads(upstream_all, hidden_pieces, pattern_down, size, True))
    input_grad = back_to_rows(
        second_product((grad_gate_pieces, grad_up_pieces), (gate_folded, up_folded), True)
    )
    delta_grad_up = core_sum(*slot_grads(token_all, grad_up_pieces, pattern_up, size, False))
    delta_grad_gate = core_sum(*slot_grads(token_all, grad_gate_pieces, pattern_gate, size, False))
    return (output, input_grad, delta_grad_gate, delta_grad_up, delta_grad_down)


def solution(mesh):
    finer = Mesh(
        mesh.devices.reshape(2, mesh.shape["row"] // 2, mesh.shape["col"] // 2, 2, 2),
        ("xl", "y", "z", "xh", "dp"),
    )
    placed = (
        P(("xl", "y", "dp"), COL),
        P(("xl", "y", "dp"), COL),
        P(COL, ROW),
        P(COL, ROW),
        P(ROW, COL),
        P(COL, ROW, None, None, None),
        P(COL, ROW, None, None, None),
        P(ROW, COL, None, None, None),
        P(COL, ROW, None),
        P(COL, ROW, None),
        P(ROW, COL, None),
    )
    return jax.shard_map(
        local,
        mesh=finer,
        in_specs=placed,
        out_specs=(
            P(("xl", "y", "dp"), COL),
            P(("xl", "y", "dp"), COL),
            P(COL, ROW, "dp", None, None),
            P(COL, ROW, "dp", None, None),
            P(ROW, COL, "dp", None, None),
        ),
        check_vma=False,
    )
```

```python
import jax
import jax.numpy as jnp
from jax import lax
from jax.experimental import pallas as pl
from jax.experimental.pallas import tpu as pltpu
from jax.sharding import Mesh
from jax.sharding import PartitionSpec as P

ROW = ("xl", "y")
COL = ("z", "xh")
BF = jnp.bfloat16
F32 = jnp.float32
STEP = 256
MIB = 1024 * 1024


def params(mib):
    return pltpu.CompilerParams(vmem_limit_bytes=mib * MIB)


def cost(flops, moved):
    return pl.CostEstimate(flops=int(flops), bytes_accessed=int(moved), transcendentals=0)


def row_gather(arrays):
    nx, ny = lax.axis_size("xl"), lax.axis_size("y")
    swap = [(i, (i + 1) % nx) for i in range(nx)]
    mine = []
    for a in arrays:
        mine += [a, lax.ppermute(a, "xl", swap)]
    block = jnp.concatenate(mine, axis=0)
    return [block] + [
        lax.ppermute(block, "y", [(i, (i + d) % ny) for i in range(ny)]) for d in range(1, ny)
    ]


def row_sum(parts):
    nx, ny = lax.axis_size("xl"), lax.axis_size("y")
    total = None
    for dx in range(nx):
        for dy in range(ny):
            to = ((lax.axis_index("xl") + dx) % nx) * ny + (lax.axis_index("y") + dy) % ny
            at = (to + nx * ny - lax.axis_index("z")) % (nx * ny)
            part = lax.dynamic_index_in_dim(parts, at, 0, keepdims=False)
            if (dx, dy) != (0, 0):
                perm = [
                    (a * ny + b, ((a + dx) % nx) * ny + (b + dy) % ny)
                    for a in range(nx)
                    for b in range(ny)
                ]
                part = lax.ppermute(part, ROW, perm)
            total = part.astype(F32) if total is None else total + part.astype(F32)
    return total


def z_shift(value, by):
    n = lax.axis_size("z")
    return lax.ppermute(value, "z", [(i, (i + by) % n) for i in range(n)])


def z_sum(partial):
    n, _, width = partial.shape
    half, far = width // 2, n // 2
    up = z_shift(partial[far, :, :half].astype(BF), 1)
    down = z_shift(partial[far, :, half:].astype(BF), -1)
    up, down = lax.optimization_barrier((up, down))
    up_term, down_term = partial[far - 1], partial[n + 1 - far]
    up_send = jnp.concatenate((up_term[:, :half] + up.astype(F32), up_term[:, half:]), axis=1)
    down_send = jnp.concatenate(
        (down_term[:, :half], down_term[:, half:] + down.astype(F32)), axis=1
    )
    for d in range(far - 1, 0, -1):
        up = z_shift(up_send.astype(BF), 1)
        down = z_shift(down_send.astype(BF), -1)
        up, down = lax.optimization_barrier((up, down))
        if d > 1:
            up_send = partial[d - 1] + up.astype(F32)
            down_send = partial[n + 1 - d] + down.astype(F32)
    return partial[0] + up.astype(F32) + down.astype(F32)


def z_gather(value, each):
    n = lax.axis_size("z")
    half, far = value.shape[1] // 2, n // 2
    chunks, below, above = {0: each(value)}, value, value
    for d in range(1, far):
        below, above = z_shift(below, 1), z_shift(above, -1)
        chunks[n - d], chunks[d] = each(below), each(above)
    left, right = each(z_shift(below[:, :half], 1)), each(z_shift(above[:, half:], -1))
    chunks[far] = jnp.concatenate((left, right), axis=1)
    return jnp.concatenate([chunks[d] for d in range(n)], axis=0)


def xh_swap(value):
    return lax.ppermute(value, "xh", [(0, 1), (1, 0)])


def halves_swapped(value):
    half = value.shape[0] // 2
    return jnp.concatenate((value[half:], value[:half]), axis=0)


def with_other_half(value):
    return jnp.concatenate((value, xh_swap(value)), axis=0)


def fold_kernel(pattern, w_ref, blocks_ref, out_ref):
    size = blocks_ref.shape[-1]
    down = out_ref.shape[0] // size
    across = out_ref.shape[1] // size
    out_ref[...] = w_ref[...]

    def one(s, carry):
        k = pattern[s]

        @pl.when(k < down * across)
        def _():
            rows = pl.ds(pl.multiple_of((k // across) * size, size), size)
            columns = pl.ds(pl.multiple_of((k % across) * size, size), size)
            total = w_ref[rows, columns].astype(F32) + blocks_ref[s].astype(F32)
            out_ref[rows, columns] = total.astype(BF)

        return carry

    lax.fori_loop(0, blocks_ref.shape[0], one, 0)


def fold(weight, blocks, pattern):
    slots, size = blocks.shape[2], blocks.shape[3]
    return pl.pallas_call(
        fold_kernel,
        out_shape=jax.ShapeDtypeStruct(weight.shape, BF),
        in_specs=[
            pl.BlockSpec(memory_space=pltpu.SMEM),
            pl.BlockSpec(memory_space=pltpu.VMEM),
            pl.BlockSpec(memory_space=pltpu.VMEM),
        ],
        out_specs=pl.BlockSpec(memory_space=pltpu.VMEM),
        compiler_params=params(8),
        cost_estimate=cost(weight.size, weight.size * 4 + blocks.size * 2),
        name="fold",
    )(pattern.reshape(-1), weight, blocks.reshape(slots, size, size))


def start_rows(blocks, wholes, sems):
    nx, ny = lax.axis_size("xl"), lax.axis_size("y")
    parts = nx * len(wholes)
    rows = blocks[0].shape[0] // parts
    half = rows // 2
    xh = lax.axis_index("xh")
    copies = []
    for d, block in enumerate(blocks):
        for p in range(parts):
            member = ((lax.axis_index("xl") + p) % nx) * ny + (lax.axis_index("y") + ny - d) % ny
            chunk = (member + nx * ny - lax.axis_index("z")) % (nx * ny)
            for h in range(2):
                to = pl.multiple_of(chunk * rows + ((h + xh) % 2) * half, half)
                copies.append(
                    pltpu.make_async_copy(
                        block.at[pl.ds(p * rows + h * half, half)],
                        wholes[p // nx].at[pl.ds(to, half)],
                        sems.at[d, p, h],
                    )
                )
    for c in copies:
        c.start()
    return copies


def first_products(blocks, rows_in_all, weights):
    n = len(blocks)
    m, depth = rows_in_all, blocks[0].shape[1]
    count = len(weights)
    width = weights[0].shape[1]

    def kernel(*refs):
        blocks_in, w, outs = refs[:n], refs[n : n + count], refs[n + count : n + 2 * count]
        turned, right, whole, sems = refs[n + 2 * count :]

        @pl.when(pl.program_id(0) == 0)
        def _():
            for c in start_rows(blocks_in, (whole, right), sems):
                c.wait()
            turned[...] = whole[...].T

        for w_ref, o_ref in zip(w, outs):
            o_ref[...] = jnp.dot(whole[...], w_ref[...], preferred_element_type=F32)

    return pl.pallas_call(
        kernel,
        grid=(width // STEP,),
        out_shape=[jax.ShapeDtypeStruct((m, width), F32)] * count
        + [jax.ShapeDtypeStruct((depth, m), BF), jax.ShapeDtypeStruct((m, depth), BF)],
        in_specs=[pl.BlockSpec(memory_space=pl.ANY)] * n
        + [pl.BlockSpec((depth, STEP), lambda i: (0, i))] * count,
        out_specs=[pl.BlockSpec((m, STEP), lambda i: (0, i))] * count
        + [pl.BlockSpec((depth, m), lambda i: (0, 0)), pl.BlockSpec((m, depth), lambda i: (0, 0))],
        scratch_shapes=[pltpu.VMEM((m, depth), BF), pltpu.SemaphoreType.DMA((n, 2 * lax.axis_size("xl"), 2))],
        compiler_params=params(12),
        cost_estimate=cost(
            2 * m * depth * width * count, count * (depth * width * 2 + m * width * 4)
        ),
        name="first_products",
    )(*blocks, *weights)


def second_products(hidden, grads, down, gate, up):
    m, depth = hidden.shape
    width = down.shape[1]
    back = (((1,), (1,)), ((), ()))

    def kernel(hidden_ref, grads_ref, down_ref, gate_ref, up_ref, out):
        def one(i, carry):
            at = pl.ds(pl.multiple_of(i * STEP, STEP), STEP)
            out[:, at] = jnp.dot(
                hidden_ref[...], down_ref[:, at], preferred_element_type=F32
            ).astype(BF)
            total = lax.dot_general(
                grads_ref[:, :depth], gate_ref[at, :], back, preferred_element_type=F32
            ) + lax.dot_general(
                grads_ref[:, depth:], up_ref[at, :], back, preferred_element_type=F32
            )
            out[:, pl.ds(pl.multiple_of(width + i * STEP, STEP), STEP)] = total.astype(BF)
            return carry

        lax.fori_loop(0, width // STEP, one, 0)

    return pl.pallas_call(
        kernel,
        out_shape=jax.ShapeDtypeStruct((m, 2 * width), BF),
        in_specs=[pl.BlockSpec(memory_space=pltpu.VMEM)] * 5,
        out_specs=pl.BlockSpec(memory_space=pltpu.VMEM),
        compiler_params=params(20),
        cost_estimate=cost(6 * m * depth * width, 6 * (depth * width + m * depth)),
        name="second_products",
    )(hidden, grads, down, gate, up)


def back_product(rows_all, weight):
    m, depth = rows_all.shape
    width = weight.shape[0]

    def kernel(rows_ref, w_ref, out_ref):
        out_ref[...] = lax.dot_general(
            rows_ref[...], w_ref[...], (((1,), (1,)), ((), ())), preferred_element_type=F32
        )

    return pl.pallas_call(
        kernel,
        grid=(width // STEP,),
        out_shape=jax.ShapeDtypeStruct((m, width), F32),
        in_specs=[
            pl.BlockSpec((m, depth), lambda i: (0, 0)),
            pl.BlockSpec((STEP, depth), lambda i: (i, 0)),
        ],
        out_specs=pl.BlockSpec((m, STEP), lambda i: (0, i)),
        compiler_params=params(8),
        cost_estimate=cost(2 * m * depth * width, depth * width * 2 + m * width * 4),
        name="back_product",
    )(rows_all, weight)


def slot_grads(left, right, pattern, size, turned, wide, first=0):
    if turned:
        narrow, m = left.shape
    else:
        m, narrow = right.shape
    slots = pattern.size
    keep = slots // 2
    blocks = wide // size
    per_narrow = narrow // size
    per_step = STEP // size

    def kernel(pattern_ref, left_ref, right_ref, mine, send, dense):
        def tile(i, carry):
            if turned:
                at = pl.ds(pl.multiple_of(first + i * STEP, STEP), STEP)
                got = jnp.dot(left_ref[...], right_ref[:, at], preferred_element_type=F32)
                for b in range(per_step):
                    dense[i * per_step + b] = got[:, b * size : (b + 1) * size]
            else:
                at = pl.ds(pl.multiple_of(i * STEP, STEP), STEP)
                got = lax.dot_general(
                    left_ref[:, at],
                    right_ref[...],
                    (((0,), (0,)), ((), ())),
                    preferred_element_type=F32,
                )
                dense[pl.ds(i * per_step, per_step)] = got.reshape(per_step, size, narrow)
            return carry

        lax.fori_loop(0, wide // STEP, tile, 0)
        core = lax.axis_index("dp")

        def pick(s):
            k = pattern_ref[s]
            live = k < blocks * per_narrow
            k = jnp.minimum(k, blocks * per_narrow - 1)
            if turned:
                a, b = k // blocks, k % blocks
                got = dense[b, pl.ds(pl.multiple_of(a * size, size), size), :]
            else:
                a, b = k // per_narrow, k % per_narrow
                got = dense[a, :, pl.ds(pl.multiple_of(b * size, size), size)]
            return jnp.where(live, got, jnp.zeros_like(got))

        def one(s, carry):
            mine[s] = pick(core * keep + s)
            send[s] = pick((1 - core) * keep + s)
            return carry

        lax.fori_loop(0, keep, one, 0)

    dense_shape = (blocks, narrow, size) if turned else (blocks, size, narrow)
    out = jax.ShapeDtypeStruct((keep, size, size), F32)
    return pl.pallas_call(
        kernel,
        out_shape=[out, out],
        in_specs=[
            pl.BlockSpec(memory_space=pltpu.SMEM),
            pl.BlockSpec(memory_space=pltpu.VMEM),
            pl.BlockSpec(memory_space=pltpu.VMEM),
        ],
        out_specs=[pl.BlockSpec(memory_space=pltpu.VMEM)] * 2,
        scratch_shapes=[pltpu.VMEM(dense_shape, F32)],
        compiler_params=params(16),
        cost_estimate=cost(2 * m * narrow * wide, m * (narrow + wide) * 2 + slots * size * size * 4),
        name="slot_grads",
    )(pattern.reshape(-1), left, right)


def core_sum(mine, send):
    got = lax.ppermute(send, "dp", [(0, 1), (1, 0)])
    total = mine + got
    return total.reshape((1, 1) + total.shape)


def local(
    tokens,
    upstream,
    w_gate,
    w_up,
    w_down,
    delta_gate,
    delta_up,
    delta_down,
    pattern_gate,
    pattern_up,
    pattern_down,
):
    size = delta_gate.shape[-1]
    nz = lax.axis_size("z")
    members = lax.axis_size("xl") * lax.axis_size("y")
    blocks = row_gather((tokens, upstream))
    gate_folded = fold(w_gate, delta_gate, pattern_gate)
    up_folded = fold(w_up, delta_up, pattern_up)
    down_folded = fold(w_down, delta_down, pattern_down)

    gate_part, up_part, token_turned, upstream_all = first_products(
        blocks, members * tokens.shape[0], (gate_folded, up_folded)
    )
    backward_part = back_product(upstream_all, down_folded)

    width = gate_part.shape[1]
    half = tokens.shape[0] // 2

    def column_sum(part):
        part = z_sum(part.reshape(nz, -1, width))
        return part + halves_swapped(xh_swap(part.astype(BF))).astype(F32)

    backward_part = backward_part.reshape(nz, -1, width)
    other = xh_swap(backward_part[:, half:].astype(BF))
    gate = column_sum(gate_part)
    up = column_sum(up_part)
    backward = z_sum(backward_part[:, :half] + other.astype(F32))
    s = jax.nn.sigmoid(gate)
    hidden = (gate * s * up).astype(BF)
    gate, up, s = gate[:half], up[:half], s[:half]
    grad_up = (backward * gate * s).astype(BF)
    grad_gate = (backward * up * s * (1.0 + gate * (1.0 - s))).astype(BF)
    hidden_all = z_gather(hidden, lambda chunk: chunk)
    grads_all = z_gather(jnp.concatenate((grad_gate, grad_up), axis=1), with_other_half)

    both = second_products(hidden_all, grads_all, down_folded, gate_folded, up_folded)
    total = row_sum(both.reshape(members, -1, both.shape[1])).astype(BF)
    total = jnp.where(lax.axis_index("xh") == 0, total, halves_swapped(total))
    output, input_grad = jnp.split(total, 2, axis=1)
    delta_grad_down = core_sum(
        *slot_grads(hidden_all, upstream_all, pattern_down, size, False, width)
    )
    delta_grad_up = core_sum(
        *slot_grads(token_turned, grads_all, pattern_up, size, True, width, width)
    )
    delta_grad_gate = core_sum(
        *slot_grads(token_turned, grads_all, pattern_gate, size, True, width, 0)
    )
    return (output, input_grad, delta_grad_gate, delta_grad_up, delta_grad_down)


def solution(mesh):
    finer = Mesh(
        mesh.devices.reshape(2, mesh.shape["row"] // 2, mesh.shape["col"] // 2, 2, 2),
        ("xl", "y", "z", "xh", "dp"),
    )
    placed = (
        P(("xl", "y", "dp"), COL),
        P(("xl", "y", "dp"), COL),
        P(COL, ROW),
        P(COL, ROW),
        P(ROW, COL),
        P(COL, ROW, None, None, None),
        P(COL, ROW, None, None, None),
        P(ROW, COL, None, None, None),
        P(COL, ROW, None),
        P(COL, ROW, None),
        P(ROW, COL, None),
    )
    return jax.shard_map(
        local,
        mesh=finer,
        in_specs=placed,
        out_specs=(
            P(("xl", "y", "dp"), COL),
            P(("xl", "y", "dp"), COL),
            P(COL, ROW, "dp", None, None),
            P(COL, ROW, "dp", None, None),
            P(ROW, COL, "dp", None, None),
        ),
        check_vma=False,
    )
```

```python
import jax
import jax.numpy as jnp
from jax import lax
from jax.experimental import pallas as pl
from jax.experimental.pallas import tpu as pltpu
from jax.sharding import Mesh
from jax.sharding import PartitionSpec as P

ROW = ("xl", "y")
COL = ("z", "xh")
BF = jnp.bfloat16
F32 = jnp.float32
STEP = 256
MIB = 1024 * 1024


def params(mib):
    return pltpu.CompilerParams(vmem_limit_bytes=mib * MIB)


def cost(flops, moved):
    return pl.CostEstimate(flops=int(flops), bytes_accessed=int(moved), transcendentals=0)


def row_gather(arrays):
    nx, ny = lax.axis_size("xl"), lax.axis_size("y")
    swap = [(i, (i + 1) % nx) for i in range(nx)]
    mine = []
    for a in arrays:
        mine += [a, lax.ppermute(a, "xl", swap)]
    block = jnp.concatenate(mine, axis=0)
    return [block] + [
        lax.ppermute(block, "y", [(i, (i + d) % ny) for i in range(ny)]) for d in range(1, ny)
    ]


def row_sum(parts):
    nx, ny = lax.axis_size("xl"), lax.axis_size("y")
    total = None
    for dx in range(nx):
        for dy in range(ny):
            to = ((lax.axis_index("xl") + dx) % nx) * ny + (lax.axis_index("y") + dy) % ny
            at = (to + nx * ny - lax.axis_index("z")) % (nx * ny)
            part = lax.dynamic_index_in_dim(parts, at, 0, keepdims=False)
            if (dx, dy) != (0, 0):
                perm = [
                    (a * ny + b, ((a + dx) % nx) * ny + (b + dy) % ny)
                    for a in range(nx)
                    for b in range(ny)
                ]
                part = lax.ppermute(part, ROW, perm)
            total = part.astype(F32) if total is None else total + part.astype(F32)
    return total


def z_shift(value, by):
    n = lax.axis_size("z")
    return lax.ppermute(value, "z", [(i, (i + by) % n) for i in range(n)])


def z_sum(partial):
    n, _, width = partial.shape
    half, far = width // 2, n // 2
    up = z_shift(partial[far, :, :half].astype(BF), 1)
    down = z_shift(partial[far, :, half:].astype(BF), -1)
    up, down = lax.optimization_barrier((up, down))
    up_term, down_term = partial[far - 1], partial[n + 1 - far]
    up_send = jnp.concatenate((up_term[:, :half] + up.astype(F32), up_term[:, half:]), axis=1)
    down_send = jnp.concatenate(
        (down_term[:, :half], down_term[:, half:] + down.astype(F32)), axis=1
    )
    for d in range(far - 1, 0, -1):
        up = z_shift(up_send.astype(BF), 1)
        down = z_shift(down_send.astype(BF), -1)
        up, down = lax.optimization_barrier((up, down))
        if d > 1:
            up_send = partial[d - 1] + up.astype(F32)
            down_send = partial[n + 1 - d] + down.astype(F32)
    return partial[0] + up.astype(F32) + down.astype(F32)


def z_gather(value, each):
    n = lax.axis_size("z")
    half, far = value.shape[1] // 2, n // 2
    chunks, below, above = {0: each(value)}, value, value
    for d in range(1, far):
        below, above = z_shift(below, 1), z_shift(above, -1)
        chunks[n - d], chunks[d] = each(below), each(above)
    left, right = each(z_shift(below[:, :half], 1)), each(z_shift(above[:, half:], -1))
    chunks[far] = jnp.concatenate((left, right), axis=1)
    return jnp.concatenate([chunks[d] for d in range(n)], axis=0)


def xh_swap(value):
    return lax.ppermute(value, "xh", [(0, 1), (1, 0)])


def halves_swapped(value):
    half = value.shape[0] // 2
    return jnp.concatenate((value[half:], value[:half]), axis=0)


def with_other_half(value):
    return jnp.concatenate((value, xh_swap(value)), axis=0)


def fold_kernel(pattern, w_ref, blocks_ref, out_ref):
    size = blocks_ref.shape[-1]
    down = out_ref.shape[0] // size
    across = out_ref.shape[1] // size
    out_ref[...] = w_ref[...]

    def one(s, carry):
        k = pattern[s]

        @pl.when(k < down * across)
        def _():
            rows = pl.ds(pl.multiple_of((k // across) * size, size), size)
            columns = pl.ds(pl.multiple_of((k % across) * size, size), size)
            total = w_ref[rows, columns].astype(F32) + blocks_ref[s].astype(F32)
            out_ref[rows, columns] = total.astype(BF)

        return carry

    lax.fori_loop(0, blocks_ref.shape[0], one, 0)


def fold(weight, blocks, pattern):
    slots, size = blocks.shape[2], blocks.shape[3]
    return pl.pallas_call(
        fold_kernel,
        out_shape=jax.ShapeDtypeStruct(weight.shape, BF),
        in_specs=[
            pl.BlockSpec(memory_space=pltpu.SMEM),
            pl.BlockSpec(memory_space=pltpu.VMEM),
            pl.BlockSpec(memory_space=pltpu.VMEM),
        ],
        out_specs=pl.BlockSpec(memory_space=pltpu.VMEM),
        compiler_params=params(8),
        cost_estimate=cost(weight.size, weight.size * 4 + blocks.size * 2),
        name="fold",
    )(pattern.reshape(-1), weight, blocks.reshape(slots, size, size))


def start_rows(blocks, wholes, sems):
    nx, ny = lax.axis_size("xl"), lax.axis_size("y")
    parts = nx * len(wholes)
    rows = blocks[0].shape[0] // parts
    half = rows // 2
    xh = lax.axis_index("xh")
    copies = []
    for d, block in enumerate(blocks):
        for p in range(parts):
            member = ((lax.axis_index("xl") + p) % nx) * ny + (lax.axis_index("y") + ny - d) % ny
            chunk = (member + nx * ny - lax.axis_index("z")) % (nx * ny)
            for h in range(2):
                to = pl.multiple_of(chunk * rows + ((h + xh) % 2) * half, half)
                copies.append(
                    pltpu.make_async_copy(
                        block.at[pl.ds(p * rows + h * half, half)],
                        wholes[p // nx].at[pl.ds(to, half)],
                        sems.at[d, p, h],
                    )
                )
    for c in copies:
        c.start()
    return copies


def first_products(blocks, rows_in_all, weights):
    n = len(blocks)
    m, depth = rows_in_all, blocks[0].shape[1]
    count = len(weights)
    width = weights[0].shape[1]

    def kernel(*refs):
        blocks_in, w, outs = refs[:n], refs[n : n + count], refs[n + count : n + 2 * count]
        turned, right, whole, sems = refs[n + 2 * count :]

        @pl.when(pl.program_id(0) == 0)
        def _():
            for c in start_rows(blocks_in, (whole, right), sems):
                c.wait()
            turned[...] = whole[...].T

        for w_ref, o_ref in zip(w, outs):
            o_ref[...] = jnp.dot(whole[...], w_ref[...], preferred_element_type=F32)

    return pl.pallas_call(
        kernel,
        grid=(width // STEP,),
        out_shape=[jax.ShapeDtypeStruct((m, width), F32)] * count
        + [jax.ShapeDtypeStruct((depth, m), BF), jax.ShapeDtypeStruct((m, depth), BF)],
        in_specs=[pl.BlockSpec(memory_space=pl.ANY)] * n
        + [pl.BlockSpec((depth, STEP), lambda i: (0, i))] * count,
        out_specs=[pl.BlockSpec((m, STEP), lambda i: (0, i))] * count
        + [pl.BlockSpec((depth, m), lambda i: (0, 0)), pl.BlockSpec((m, depth), lambda i: (0, 0))],
        scratch_shapes=[pltpu.VMEM((m, depth), BF), pltpu.SemaphoreType.DMA((n, 2 * lax.axis_size("xl"), 2))],
        compiler_params=params(12),
        cost_estimate=cost(
            2 * m * depth * width * count, count * (depth * width * 2 + m * width * 4)
        ),
        name="first_products",
    )(*blocks, *weights)


def second_products(hidden, grads, down, gate, up):
    m, depth = hidden.shape
    width = down.shape[1]
    back = (((1,), (1,)), ((), ()))

    def kernel(hidden_ref, grads_ref, down_ref, gate_ref, up_ref, out):
        def one(i, carry):
            at = pl.ds(pl.multiple_of(i * STEP, STEP), STEP)
            out[:, at] = jnp.dot(
                hidden_ref[...], down_ref[:, at], preferred_element_type=F32
            ).astype(BF)
            total = lax.dot_general(
                grads_ref[:, :depth], gate_ref[at, :], back, preferred_element_type=F32
            ) + lax.dot_general(
                grads_ref[:, depth:], up_ref[at, :], back, preferred_element_type=F32
            )
            out[:, pl.ds(pl.multiple_of(width + i * STEP, STEP), STEP)] = total.astype(BF)
            return carry

        lax.fori_loop(0, width // STEP, one, 0)

    return pl.pallas_call(
        kernel,
        out_shape=jax.ShapeDtypeStruct((m, 2 * width), BF),
        in_specs=[pl.BlockSpec(memory_space=pltpu.VMEM)] * 5,
        out_specs=pl.BlockSpec(memory_space=pltpu.VMEM),
        compiler_params=params(20),
        cost_estimate=cost(6 * m * depth * width, 6 * (depth * width + m * depth)),
        name="second_products",
    )(hidden, grads, down, gate, up)


def back_product(rows_all, weight):
    m, depth = rows_all.shape
    width = weight.shape[0]

    def kernel(rows_ref, w_ref, out_ref):
        out_ref[...] = lax.dot_general(
            rows_ref[...], w_ref[...], (((1,), (1,)), ((), ())), preferred_element_type=F32
        )

    return pl.pallas_call(
        kernel,
        grid=(width // STEP,),
        out_shape=jax.ShapeDtypeStruct((m, width), F32),
        in_specs=[
            pl.BlockSpec((m, depth), lambda i: (0, 0)),
            pl.BlockSpec((STEP, depth), lambda i: (i, 0)),
        ],
        out_specs=pl.BlockSpec((m, STEP), lambda i: (0, i)),
        compiler_params=params(8),
        cost_estimate=cost(2 * m * depth * width, depth * width * 2 + m * width * 4),
        name="back_product",
    )(rows_all, weight)


def slot_grads(left, right, pattern, size, turned, wide, first=0):
    if turned:
        narrow, m = left.shape
    else:
        m, narrow = right.shape
    slots = pattern.size
    keep = slots // 2
    blocks = wide // size
    per_narrow = narrow // size
    per_step = STEP // size

    def kernel(pattern_ref, left_ref, right_ref, mine, send, dense):
        def tile(i, carry):
            if turned:
                at = pl.ds(pl.multiple_of(first + i * STEP, STEP), STEP)
                got = jnp.dot(left_ref[...], right_ref[:, at], preferred_element_type=F32)
                for b in range(per_step):
                    dense[i * per_step + b] = got[:, b * size : (b + 1) * size]
            else:
                at = pl.ds(pl.multiple_of(i * STEP, STEP), STEP)
                got = lax.dot_general(
                    left_ref[:, at],
                    right_ref[...],
                    (((0,), (0,)), ((), ())),
                    preferred_element_type=F32,
                )
                dense[pl.ds(i * per_step, per_step)] = got.reshape(per_step, size, narrow)
            return carry

        lax.fori_loop(0, wide // STEP, tile, 0)
        core = lax.axis_index("dp")

        def pick(s):
            k = pattern_ref[s]
            live = k < blocks * per_narrow
            k = jnp.minimum(k, blocks * per_narrow - 1)
            if turned:
                a, b = k // blocks, k % blocks
                got = dense[b, pl.ds(pl.multiple_of(a * size, size), size), :]
            else:
                a, b = k // per_narrow, k % per_narrow
                got = dense[a, :, pl.ds(pl.multiple_of(b * size, size), size)]
            return jnp.where(live, got, jnp.zeros_like(got))

        def one(s, carry):
            mine[s] = pick(core * keep + s)
            send[s] = pick((1 - core) * keep + s)
            return carry

        lax.fori_loop(0, keep, one, 0)

    dense_shape = (blocks, narrow, size) if turned else (blocks, size, narrow)
    out = jax.ShapeDtypeStruct((keep, size, size), F32)
    return pl.pallas_call(
        kernel,
        out_shape=[out, out],
        in_specs=[
            pl.BlockSpec(memory_space=pltpu.SMEM),
            pl.BlockSpec(memory_space=pltpu.VMEM),
            pl.BlockSpec(memory_space=pltpu.VMEM),
        ],
        out_specs=[pl.BlockSpec(memory_space=pltpu.VMEM)] * 2,
        scratch_shapes=[pltpu.VMEM(dense_shape, F32)],
        compiler_params=params(16),
        cost_estimate=cost(2 * m * narrow * wide, m * (narrow + wide) * 2 + slots * size * size * 4),
        name="slot_grads",
    )(pattern.reshape(-1), left, right)


def core_sum(mine, send):
    got = lax.ppermute(send, "dp", [(0, 1), (1, 0)])
    total = mine + got
    return total.reshape((1, 1) + total.shape)


def local(
    tokens,
    upstream,
    w_gate,
    w_up,
    w_down,
    delta_gate,
    delta_up,
    delta_down,
    pattern_gate,
    pattern_up,
    pattern_down,
):
    size = delta_gate.shape[-1]
    nz = lax.axis_size("z")
    members = lax.axis_size("xl") * lax.axis_size("y")
    blocks = row_gather((tokens, upstream))
    gate_folded = fold(w_gate, delta_gate, pattern_gate)
    up_folded = fold(w_up, delta_up, pattern_up)
    down_folded = fold(w_down, delta_down, pattern_down)

    gate_part, up_part, token_turned, upstream_all = first_products(
        blocks, members * tokens.shape[0], (gate_folded, up_folded)
    )
    backward_part = back_product(upstream_all, down_folded)

    width = gate_part.shape[1]
    half = tokens.shape[0] // 2

    def column_sum(part):
        part = z_sum(part.reshape(nz, -1, width))
        return part + halves_swapped(xh_swap(part.astype(BF))).astype(F32)

    backward_part = backward_part.reshape(nz, -1, width)
    other = xh_swap(backward_part[:, half:].astype(BF))
    gate = column_sum(gate_part)
    up = column_sum(up_part)
    backward = z_sum(backward_part[:, :half] + other.astype(F32))
    s = jax.nn.sigmoid(gate)
    hidden = (gate * s * up).astype(BF)
    gate, up, s = gate[:half], up[:half], s[:half]
    grad_up = (backward * gate * s).astype(BF)
    grad_gate = (backward * up * s * (1.0 + gate * (1.0 - s))).astype(BF)
    hidden_all = z_gather(hidden, lambda chunk: chunk)
    grads_all = z_gather(jnp.concatenate((grad_gate, grad_up), axis=1), with_other_half)

    both = second_products(hidden_all, grads_all, down_folded, gate_folded, up_folded)
    total = row_sum(both.reshape(members, -1, both.shape[1])).astype(BF)
    total = jnp.where(lax.axis_index("xh") == 0, total, halves_swapped(total))
    output, input_grad = jnp.split(total, 2, axis=1)
    delta_grad_down = core_sum(
        *slot_grads(hidden_all, upstream_all, pattern_down, size, False, width)
    )
    gate_mine, gate_send = slot_grads(
        token_turned, grads_all, pattern_gate, size, True, width, 0
    )
    up_mine, up_send = slot_grads(
        token_turned, grads_all, pattern_up, size, True, width, width
    )
    got = lax.ppermute(jnp.concatenate((gate_send, up_send), axis=0), "dp", [(0, 1), (1, 0)])
    keep = gate_mine.shape[0]
    delta_grad_gate = (gate_mine + got[:keep])[None, None]
    delta_grad_up = (up_mine + got[keep:])[None, None]
    return (output, input_grad, delta_grad_gate, delta_grad_up, delta_grad_down)


def solution(mesh):
    finer = Mesh(
        mesh.devices.reshape(2, mesh.shape["row"] // 2, mesh.shape["col"] // 2, 2, 2),
        ("xl", "y", "z", "xh", "dp"),
    )
    placed = (
        P(("xl", "y", "dp"), COL),
        P(("xl", "y", "dp"), COL),
        P(COL, ROW),
        P(COL, ROW),
        P(ROW, COL),
        P(COL, ROW, None, None, None),
        P(COL, ROW, None, None, None),
        P(ROW, COL, None, None, None),
        P(COL, ROW, None),
        P(COL, ROW, None),
        P(ROW, COL, None),
    )
    return jax.shard_map(
        local,
        mesh=finer,
        in_specs=placed,
        out_specs=(
            P(("xl", "y", "dp"), COL),
            P(("xl", "y", "dp"), COL),
            P(COL, ROW, "dp", None, None),
            P(COL, ROW, "dp", None, None),
            P(ROW, COL, "dp", None, None),
        ),
        check_vma=False,
    )
```
